512 devices in a mesh: grid: 64 (over x, z, core), band: 8 (over y).
Axes of the slice: x: 4, y: 8, z: 8, core: 2. Of those that a mesh axis runs over, the one named last changes fastest.
Arguments:
- orbitals: float32 [128, 256, 16, 128], P('band', 'grid'), may hold values from -16 to 16
- potential: float32 [256, 16, 128], P('grid'), may hold values from 0 to 2
Outputs:
- filtered: float32 [128, 256, 16, 128], P('band', 'grid')
- intersection: float32 [128, 128], P('band')
- hamiltonian: float32 [128, 128], P('band')
The draws below stay inside these ranges and needn't reach their ends.
All inputs are finite; a program needn't handle non-finite values.
Results may differ from the reference program's by a relative error of at most 0.00011.
Values sent between devices are 32-bit elements; how exact they have to be, the bound alone decides.
No kernel may reach another device: no remote copies, remote signals or barrier semaphores. Data moves between devices by JAX's collectives and lax.ppermute only.
A program may use at most 64 MiB of HBM per device.

```python
import math
import jax
import jax.numpy as jnp
from jax import lax

NB = 16
NX = 16
NY = 128
ORBS = 128
NZ = 256
N_BAND = 8


def draw_orbitals(key, part):
    key_mix = jax.random.fold_in(key, 11)
    key_plane = jax.random.fold_in(key, 12)
    key_orbit = jax.random.fold_in(key, 13)
    key_fields = jax.random.fold_in(key, 14)
    plane_spread = 0.7
    orbit_spread = 0.5
    mixing = jax.random.normal(key_mix, (ORBS, ORBS), jnp.float32) * (0.8 / math.sqrt(ORBS))
    mixing = mixing + 0.6 * jnp.eye(ORBS, dtype=jnp.float32)
    plane_scale = jnp.exp(jax.random.uniform(key_plane, (NZ,), jnp.float32, -plane_spread, plane_spread))
    orbit_scale = jnp.exp(jax.random.uniform(key_orbit, (ORBS,), jnp.float32, -orbit_spread, orbit_spread))

    def add_field(index, total):
        field_key = jax.random.fold_in(key_fields, index)
        field = jnp.clip(jax.random.normal(field_key, (NZ, NX, NY), jnp.float32), -6.0, 6.0)
        column = lax.dynamic_slice_in_dim(mixing, index, 1, 1)
        return total + column[:, :, None, None] * field[None]
    total = lax.fori_loop(0, ORBS, add_field, jnp.zeros((ORBS, NZ, NX, NY), jnp.float32))
    scaled = total * orbit_scale[:, None, None, None] * plane_scale[None, :, None, None]
    return jnp.clip(scaled, -16.0, 16.0)


def shard_levels(own_key, shape, pieces, low, top_value):
    factor_of = 1.0
    for dim, parts in pieces:
        draws = jax.random.uniform(jax.random.fold_in(jax.random.fold_in(own_key, 6), dim), (parts,), jnp.float32, low / len(pieces), top_value / len(pieces))
        factor_of = factor_of * jnp.repeat(jnp.exp(draws), shape[dim] // parts).reshape((-1,) + (1,) * (len(shape) - 1 - dim))
    return factor_of


def setup_inputs(seed: int = 0) -> dict:
    streams_of = jax.random.split(jax.random.key(seed), 3)
    orbitals = draw_orbitals(jax.random.fold_in(streams_of[2], 71), 0)
    potential = jnp.clip(2.0 * jax.random.uniform(streams_of[1], (NZ, NX, NY), jnp.float32) ** shard_levels(streams_of[1], (NZ, NX, NY), ((0, 64),), -0.2, 0.2), 0.0, 2.0)
    return {"orbitals": orbitals, "potential": potential}


SHIFT_MID = 6.5
HALF_WIDTH = 3.5


def stencil(field, axis_id):
    return (-jnp.roll(field, 2, axis_id) + 16.0 * jnp.roll(field, 1, axis_id) - 30.0 * field
            + 16.0 * jnp.roll(field, -1, axis_id) - jnp.roll(field, -2, axis_id)) / 12.0


def hamilton(field, potential):
    laplacian = stencil(field, 1) + stencil(field, 2) + stencil(field, 3)
    return -0.5 * laplacian + potential[None] * field


def filter_block(block, potential):
    prior = block
    current = (hamilton(block, potential) - SHIFT_MID * block) / HALF_WIDTH
    for repeat in range(3):
        following = 2.0 * (hamilton(current, potential) - SHIFT_MID * current) / HALF_WIDTH - prior
        prior, current = current, following
    return current, hamilton(current, potential)


def reference(orbitals, potential):
    blocks = orbitals.reshape(N_BAND, NB, NZ, NX, NY)
    filtered, images = lax.map(lambda block: filter_block(block, potential), blocks)
    cells = NX * NY * NZ
    flat = filtered.reshape(ORBS, -1)
    image_flat = images.reshape(ORBS, -1)
    intersection = jnp.dot(flat, flat.T, precision=lax.Precision.HIGHEST, preferred_element_type=jnp.float32) / cells
    hamiltonian = jnp.dot(flat, image_flat.T, precision=lax.Precision.HIGHEST, preferred_element_type=jnp.float32) / cells
    return filtered.reshape(ORBS, NZ, NX, NY), intersection, hamiltonian
```

```python
import jax
import jax.numpy as jnp
from jax import lax
from jax.experimental import pallas as pl
from jax.experimental.pallas import tpu as pltpu
from jax.sharding import Mesh, PartitionSpec as P

SHIFT_MID = 6.5
HALF_WIDTH = 3.5
DIAG = 3.0 * 30.0 / 24.0
NEAR = -16.0 / 24.0
FAR = 1.0 / 24.0
GRID = ("x", "z", "core")
VMEM = pl.BlockSpec(memory_space=pltpu.VMEM)
LIMIT = pltpu.CompilerParams(vmem_limit_bytes=24 * 1024 * 1024)


def ring_shift(size, by):
    return [(i, (i + by) % size) for i in range(size)]


def scaled_op(padded, diag):
    mid = padded[2:-2]
    rows, lanes = mid.shape[1], mid.shape[2]
    near = padded[1:-3] + padded[3:-1]
    far = padded[:-4] + padded[4:]
    near = near + (pltpu.roll(mid, 1, 1) + pltpu.roll(mid, rows - 1, 1))
    far = far + (pltpu.roll(mid, 2, 1) + pltpu.roll(mid, rows - 2, 1))
    near = near + (pltpu.roll(mid, 1, 2) + pltpu.roll(mid, lanes - 1, 2))
    far = far + (pltpu.roll(mid, 2, 2) + pltpu.roll(mid, lanes - 2, 2))
    return diag * mid + (NEAR / HALF_WIDTH) * near + (FAR / HALF_WIDTH) * far


def scaled_diag(vlo, vown, vhi):
    v = jnp.concatenate([vlo[...], vown[...], vhi[...]], axis=0)
    return (v + (DIAG - SHIFT_MID)) / HALF_WIDTH


def stage_one(flo, fown, fhi, vlo, vown, vhi, out):
    diag = scaled_diag(vlo, vown, vhi)

    def step(o, carry):
        f = jnp.concatenate([flo[o], fown[o], fhi[o]], axis=0)
        first = scaled_op(f, diag)
        out[o] = 2.0 * scaled_op(first, diag[2:-2]) - fown[o]
        return carry

    lax.fori_loop(0, fown.shape[0], step, 0)


def stage_two(glo, gown, ghi, fown, vlo, vown, vhi, out, edge):
    diag = scaled_diag(vlo, vown, vhi)

    def step(o, carry):
        g = jnp.concatenate([glo[o], gown[o], ghi[o]], axis=0)
        first = scaled_op(g, diag)
        u = 4.0 * scaled_op(first, diag[2:-2]) - 2.0 * gown[o] - fown[o]
        out[o] = u
        edge[o] = u[:2]
        return carry

    lax.fori_loop(0, fown.shape[0], step, 0)


def stage_half(uown, unext, vown, out):
    orbs, planes, rows, lanes = uown.shape
    half_diag = 0.5 * (vown[...] + DIAG)

    def step(o, carry):
        u = uown[o]
        up = jnp.concatenate([u, unext[o]], axis=0)
        near = up[1:-1] + pltpu.roll(u, rows - 1, 1) + pltpu.roll(u, lanes - 1, 2)
        far = up[2:] + pltpu.roll(u, rows - 2, 1) + pltpu.roll(u, lanes - 2, 2)
        w = half_diag * u + NEAR * near + FAR * far
        for plane in range(planes):
            for part in range(rows // 8):
                peer = plane * (rows // 8) + part
                out[peer, 0, :, pl.ds(o, 1), :] = u[plane, part * 8 : part * 8 + 8][:, None, :]
                out[peer, 1, :, pl.ds(o, 1), :] = w[plane, part * 8 : part * 8 + 8][:, None, :]
        return carry

    lax.fori_loop(0, orbs, step, 0)


def gram(blocks, out):
    bands, _, rows, orbs, lanes = blocks.shape
    total = bands * orbs
    dims = (((1,), (1,)), ((), ()))

    def dot(a, b):
        return lax.dot_general(a, b, dims, precision=lax.Precision.HIGHEST, preferred_element_type=jnp.float32)

    over = jnp.zeros((total, total), jnp.float32)
    half = jnp.zeros((total, total), jnp.float32)
    for row in range(rows):
        f = blocks[:, 0, row].reshape(total, lanes)
        w = blocks[:, 1, row].reshape(total, lanes)
        over = over + dot(f, f)
        half = half + dot(f, w)
    ham = half + half.T
    out[:, 0] = over.reshape(bands, orbs, total)
    out[:, 1] = ham.reshape(bands, orbs, total)


def call(body, out_shapes, *args):
    return pl.pallas_call(
        body,
        out_shape=[jax.ShapeDtypeStruct(s, jnp.float32) for s in out_shapes],
        in_specs=[VMEM] * len(args),
        out_specs=[VMEM] * len(out_shapes),
        compiler_params=LIMIT,
    )(*args)


def per_device(orbitals, potential):
    orbs, planes, rows, lanes = orbitals.shape
    slabs = lax.axis_size(GRID)
    bands = lax.axis_size("y")
    cells_all = slabs * planes * rows * lanes
    up, down = ring_shift(slabs, 1), ring_shift(slabs, -1)

    flo = lax.ppermute(orbitals, GRID, up)
    fhi = lax.ppermute(orbitals, GRID, down)
    vlo = lax.ppermute(potential[planes - 2 :], GRID, up)
    vhi = lax.ppermute(potential[:2], GRID, down)
    (g,) = call(stage_one, [orbitals.shape], flo, orbitals, fhi, vlo, potential, vhi)

    glo = lax.ppermute(g, GRID, up)
    ghi = lax.ppermute(g, GRID, down)
    u, edge = call(
        stage_two, [orbitals.shape, (orbs, 2, rows, lanes)], glo, g, ghi, orbitals, vlo, potential, vhi
    )

    unext = lax.ppermute(edge, GRID, down)
    (send,) = call(stage_half, [(bands, 2, planes * rows // bands, orbs, lanes)], u, unext, potential)
    got = lax.all_to_all(send, "y", 0, 0, tiled=True)
    (part,) = call(gram, [(bands, 2, orbs, bands * orbs)], got)

    first = ("y", "x", "core")
    pieces = lax.axis_size(first)
    flat = part.reshape(pieces, -1, bands * orbs)
    mine = lax.all_to_all(flat, first, 0, 0, tiled=True).sum(0)
    spread = jnp.broadcast_to(mine[None], (slabs, *mine.shape))
    back = lax.all_to_all(spread, GRID, 0, 0, tiled=True)
    nx, nz, nc = (lax.axis_size(a) for a in GRID)
    both = back.reshape(nx, nz, nc, *mine.shape).sum(1) / cells_all
    both = both.reshape(2, orbs, bands * orbs)
    return u, both[0], both[1]


def solution(mesh):
    devices = mesh.devices.reshape(4, 8, 2, 8)
    fine = Mesh(devices, ("x", "z", "core", "y"))
    in_specs = (P("y", GRID, None, None), P(GRID, None, None))
    out_specs = (P("y", GRID, None, None), P("y", None), P("y", None))
    return jax.shard_map(per_device, mesh=fine, in_specs=in_specs, out_specs=out_specs, check_vma=False)
```

```python
import jax
import jax.numpy as jnp
from jax import lax
from jax.experimental import pallas as pl
from jax.experimental.pallas import tpu as pltpu
from jax.sharding import Mesh, PartitionSpec as P

SHIFT_MID = 6.5
HALF_WIDTH = 3.5
DIAG = 3.0 * 30.0 / 24.0
NEAR = -16.0 / 24.0
FAR = 1.0 / 24.0
GRID = ("x", "z", "core")
VMEM = pl.BlockSpec(memory_space=pltpu.VMEM)
LIMIT = pltpu.CompilerParams(vmem_limit_bytes=24 * 1024 * 1024)


def ring_shift(size, by):
    return [(i, (i + by) % size) for i in range(size)]


def scaled_op(padded, diag):
    mid = padded[2:-2]
    rows, lanes = mid.shape[1], mid.shape[2]
    near = padded[1:-3] + padded[3:-1]
    far = padded[:-4] + padded[4:]
    near = near + (pltpu.roll(mid, 1, 1) + pltpu.roll(mid, rows - 1, 1))
    far = far + (pltpu.roll(mid, 2, 1) + pltpu.roll(mid, rows - 2, 1))
    near = near + (pltpu.roll(mid, 1, 2) + pltpu.roll(mid, lanes - 1, 2))
    far = far + (pltpu.roll(mid, 2, 2) + pltpu.roll(mid, lanes - 2, 2))
    return diag * mid + (NEAR / HALF_WIDTH) * near + (FAR / HALF_WIDTH) * far


def by_core(run, on, off):
    core = lax.axis_index("core")
    pl.when(core == 0)(lambda: run(off, on))
    pl.when(core == 1)(lambda: run(on, off))


def stage_one(own, on, off, out, diag):
    orbs = own.shape[0] - 1

    def run(lo, hi):
        v = jnp.concatenate([lo[orbs, 2:], own[orbs], hi[orbs, :2]], axis=0)
        diag[...] = (v + (DIAG - SHIFT_MID)) / HALF_WIDTH

        def step(o, carry):
            f = jnp.concatenate([lo[o], own[o], hi[o]], axis=0)
            first = scaled_op(f, diag[...])
            out[o] = 2.0 * scaled_op(first, diag[2:-2]) - own[o]
            return carry

        lax.fori_loop(0, orbs, step, 0)

    by_core(run, on, off)


def stage_two(gown, on, off, fown, diag, out, edge):
    def run(lo, hi):
        def step(o, carry):
            g = jnp.concatenate([lo[o], gown[o], hi[o]], axis=0)
            first = scaled_op(g, diag[...])
            u = 4.0 * scaled_op(first, diag[2:-2]) - 2.0 * gown[o] - fown[o]
            out[o] = u
            edge[o] = u[:2]
            return carry

        lax.fori_loop(0, gown.shape[0], step, 0)

    by_core(run, on, off)


def stage_half(uown, unext, diag, out):
    orbs, planes, rows, lanes = uown.shape
    half_diag = 0.5 * (HALF_WIDTH * diag[2:-2] + SHIFT_MID)

    def step(o, carry):
        u = uown[o]
        up = jnp.concatenate([u, unext[o]], axis=0)
        near = up[1:-1] + pltpu.roll(u, rows - 1, 1) + pltpu.roll(u, lanes - 1, 2)
        far = up[2:] + pltpu.roll(u, rows - 2, 1) + pltpu.roll(u, lanes - 2, 2)
        w = half_diag * u + NEAR * near + FAR * far
        for plane in range(planes):
            for part in range(rows // 8):
                peer = plane * (rows // 8) + part
                out[peer, 0, :, pl.ds(o, 1), :] = u[plane, part * 8 : part * 8 + 8][:, None, :]
                out[peer, 1, :, pl.ds(o, 1), :] = w[plane, part * 8 : part * 8 + 8][:, None, :]
        return carry

    lax.fori_loop(0, orbs, step, 0)


def gram(blocks, out):
    bands, _, rows, orbs, lanes = blocks.shape
    total = bands * orbs
    dims = (((1,), (1,)), ((), ()))

    def dot(a, b):
        return lax.dot_general(a, b, dims, precision=lax.Precision.HIGHEST, preferred_element_type=jnp.float32)

    over = jnp.zeros((total, total), jnp.float32)
    half = jnp.zeros((total, total), jnp.float32)
    for row in range(rows):
        f = blocks[:, 0, row].reshape(total, lanes)
        w = blocks[:, 1, row].reshape(total, lanes)
        over = over + dot(f, f)
        half = half + dot(f, w)
    ham = half + half.T
    out[:, 0] = over.reshape(bands, orbs, total)
    out[:, 1] = ham.reshape(bands, orbs, total)


def call(body, out_shapes, *args):
    return pl.pallas_call(
        body,
        out_shape=[jax.ShapeDtypeStruct(s, jnp.float32) for s in out_shapes],
        in_specs=[VMEM] * len(args),
        out_specs=[VMEM] * len(out_shapes),
        compiler_params=LIMIT,
    )(*args)


def per_device(orbitals, potential):
    orbs, planes, rows, lanes = orbitals.shape
    slabs = lax.axis_size(GRID)
    bands = lax.axis_size("y")
    cells_all = slabs * planes * rows * lanes
    down = ring_shift(slabs, -1)
    outer = [(i, (i + (1 if i % 2 else -1)) % slabs) for i in range(slabs)]

    def both_sides(slab):
        off = lax.ppermute(slab, GRID, outer)
        return lax.ppermute(slab, "core", [(0, 1), (1, 0)]), off

    slab = jnp.concatenate([orbitals, potential[None]], axis=0)
    g, diag = call(stage_one, [orbitals.shape, (planes + 4, rows, lanes)], slab, *both_sides(slab))
    u, edge = call(
        stage_two, [orbitals.shape, (orbs, 2, rows, lanes)], g, *both_sides(g), slab, diag
    )

    unext = lax.ppermute(edge, GRID, down)
    (send,) = call(stage_half, [(bands, 2, planes * rows // bands, orbs, lanes)], u, unext, diag)
    got = lax.all_to_all(send, "y", 0, 0, tiled=True)
    (part,) = call(gram, [(bands, 2, orbs, bands * orbs)], got)

    first = ("y", "x", "core")
    pieces = lax.axis_size(first)
    flat = part.reshape(pieces, -1, bands * orbs)
    mine = lax.all_to_all(flat, first, 0, 0, tiled=True).sum(0)
    spread = jnp.broadcast_to(mine[None], (slabs, *mine.shape))
    back = lax.all_to_all(spread, GRID, 0, 0, tiled=True)
    nx, nz, nc = (lax.axis_size(a) for a in GRID)
    both = back.reshape(nx, nz, nc, *mine.shape).sum(1) / cells_all
    both = both.reshape(2, orbs, bands * orbs)
    return u, both[0], both[1]


def solution(mesh):
    devices = mesh.devices.reshape(4, 8, 2, 8)
    fine = Mesh(devices, ("x", "z", "core", "y"))
    in_specs = (P("y", GRID, None, None), P(GRID, None, None))
    out_specs = (P("y", GRID, None, None), P("y", None), P("y", None))
    return jax.shard_map(per_device, mesh=fine, in_specs=in_specs, out_specs=out_specs, check_vma=False)
```

```python
import jax
import jax.numpy as jnp
from jax import lax
from jax.experimental import pallas as pl
from jax.experimental.pallas import tpu as pltpu
from jax.sharding import Mesh, PartitionSpec as P

SHIFT_MID = 6.5
HALF_WIDTH = 3.5
DIAG = 3.0 * 30.0 / 24.0
NEAR = -16.0 / 24.0
FAR = 1.0 / 24.0
GRID = ("x", "z", "core")
VMEM = pl.BlockSpec(memory_space=pltpu.VMEM)
LIMIT = pltpu.CompilerParams(vmem_limit_bytes=24 * 1024 * 1024)


def ring_shift(size, by):
    return [(i, (i + by) % size) for i in range(size)]


def scaled_op(padded, diag):
    mid = padded[2:-2]
    rows, lanes = mid.shape[1], mid.shape[2]
    near = padded[1:-3] + padded[3:-1]
    far = padded[:-4] + padded[4:]
    near = near + (pltpu.roll(mid, 1, 1) + pltpu.roll(mid, rows - 1, 1))
    far = far + (pltpu.roll(mid, 2, 1) + pltpu.roll(mid, rows - 2, 1))
    near = near + (pltpu.roll(mid, 1, 2) + pltpu.roll(mid, lanes - 1, 2))
    far = far + (pltpu.roll(mid, 2, 2) + pltpu.roll(mid, lanes - 2, 2))
    return diag * mid + (NEAR / HALF_WIDTH) * near + (FAR / HALF_WIDTH) * far


def by_core(run, on, off):
    core = lax.axis_index("core")
    pl.when(core == 0)(lambda: run(off, on))
    pl.when(core == 1)(lambda: run(on, off))


def stage_one(own, on, off, out, diag):
    orbs = own.shape[0] - 1

    def run(lo, hi):
        v = jnp.concatenate([lo[orbs, 2:], own[orbs], hi[orbs, :2]], axis=0)
        diag[...] = (v + (DIAG - SHIFT_MID)) / HALF_WIDTH

        def step(o, carry):
            f = jnp.concatenate([lo[o], own[o], hi[o]], axis=0)
            first = scaled_op(f, diag[...])
            out[o] = 2.0 * scaled_op(first, diag[2:-2]) - own[o]
            return carry

        lax.fori_loop(0, orbs, step, 0)

    by_core(run, on, off)


def stage_two(gown, on, off, fown, diag, out, send, half_diag):
    orbs, planes, rows, lanes = gown.shape
    peers, depth, octet, _ = send.shape
    chunk = lanes // peers
    half = 0.5 * (HALF_WIDTH * diag[2:-2] + SHIFT_MID)
    half_diag[...] = jnp.concatenate([half.reshape(planes * rows, lanes)] * 2, axis=0).T

    def run(lo, hi):
        def step(p, carry):
            pair = []
            for o in (p, p + octet):
                g = jnp.concatenate([lo[o], gown[o], hi[o]], axis=0)
                first = scaled_op(g, diag[...])
                u = 4.0 * scaled_op(first, diag[2:-2]) - 2.0 * gown[o] - fown[o]
                out[o] = u
                pair.append(u.reshape(planes * rows, lanes))
            lines = jnp.concatenate(pair, axis=0).T
            for k in range(peers):
                at = (k + 1) % peers * chunk
                send[k, :chunk, pl.ds(p, 1), :] = lines[k * chunk : (k + 1) * chunk][:, None, :]
                send[k, chunk:, pl.ds(p, 1), :] = lines[at : at + depth - chunk][:, None, :]
            return carry

        lax.fori_loop(0, octet, step, 0)

    by_core(run, on, off)


def lane_ids(like):
    return lax.broadcasted_iota(jnp.int32, like.shape, 2)


def pack_edge(got, out):
    for j in range(out.shape[0]):
        a, b = got[:, 2 * j], got[:, 2 * j + 1]
        out[j] = jnp.where(lane_ids(a) % 64 < 32, a, pltpu.roll(b, 32, 2))


def split(x):
    high = x.astype(jnp.bfloat16)
    return high, (x - high.astype(jnp.float32)).astype(jnp.bfloat16)


def dot3(a, b):
    dims = (((1,), (1,)), ((), ()))
    (ah, al), (bh, bl) = a, b
    parts = [
        lax.dot_general(x, y, dims, preferred_element_type=jnp.float32) for x, y in ((ah, bh), (ah, bl), (al, bh))
    ]
    return parts[0] + (parts[1] + parts[2])


def orbital_rows(a, b):
    low = lane_ids(a) < 64
    top = jnp.where(low, a, pltpu.roll(b, 64, 2))
    end = jnp.where(low, pltpu.roll(a, 64, 2), b)
    return jnp.stack([top, end], axis=1).reshape(-1, a.shape[-1])


def gram_own(got, half_diag, over, half):
    bands, depth, octet, _ = got.shape
    start = pl.multiple_of(lax.axis_index("y") * (depth - 2), 16)
    x = lane_ids(got[:, 0]) % 16
    z = lane_ids(got[:, 0]) % 64 // 16

    def one_sided(y):
        u = got[:, y]
        near = got[:, y + 1] + jnp.where(x < 15, pltpu.roll(u, 127, 2), pltpu.roll(u, 15, 2))
        far = got[:, y + 2] + jnp.where(x < 14, pltpu.roll(u, 126, 2), pltpu.roll(u, 14, 2))
        near = near + jnp.where(z < 3, pltpu.roll(u, 112, 2), 0.0)
        far = far + jnp.where(z < 2, pltpu.roll(u, 96, 2), 0.0)
        return half_diag[pl.ds(start + y, 1), :][None] * u + NEAR * near + FAR * far

    total_over, total_half = 0.0, 0.0
    for y in range(0, depth - 2, 2):
        u = split(orbital_rows(got[:, y], got[:, y + 1]))
        w = split(orbital_rows(one_sided(y), one_sided(y + 1)))
        total_over = total_over + dot3(u, u)
        total_half = total_half + dot3(u, w)
    over[...] = total_over
    half[...] = total_half


def gram_edge(got, edge, over, half, out):
    bands, depth, octet, _ = got.shape
    z = lane_ids(edge[0]) % 64 // 16
    total = half[...]
    for j in range(edge.shape[0]):
        e = edge[j]
        by_y = []
        for near, far in ((48, 32), (16, 0)):
            one = jnp.where(z == 3, pltpu.roll(e, near, 2), 0.0)
            two = jnp.where(z >= 2, pltpu.roll(e, far, 2) if far else e, 0.0)
            by_y.append(NEAR * one + FAR * two)
        u = split(orbital_rows(got[:, 2 * j], got[:, 2 * j + 1]))
        total = total + dot3(u, split(orbital_rows(*by_y)))
    out[:, 0] = over[...].reshape(bands, -1, total.shape[-1])
    out[:, 1] = (total + total.T).reshape(bands, -1, total.shape[-1])


def call(body, out_shapes, *args, flops=0):
    return pl.pallas_call(
        body,
        out_shape=[jax.ShapeDtypeStruct(s, jnp.float32) for s in out_shapes],
        in_specs=[VMEM] * len(args),
        out_specs=[VMEM] * len(out_shapes),
        compiler_params=LIMIT,
        cost_estimate=pl.CostEstimate(flops=flops, bytes_accessed=1 << 20, transcendentals=0),
    )(*args)


def per_device(orbitals, potential):
    orbs, planes, rows, lanes = orbitals.shape
    slabs = lax.axis_size(GRID)
    bands = lax.axis_size("y")
    cells_all = slabs * planes * rows * lanes
    down = ring_shift(slabs, -1)
    outer = [(i, (i + (1 if i % 2 else -1)) % slabs) for i in range(slabs)]

    def both_sides(slab):
        off = lax.ppermute(slab, GRID, outer)
        return lax.ppermute(slab, "core", [(0, 1), (1, 0)]), off

    slab = jnp.concatenate([orbitals, potential[None]], axis=0)
    g, diag = call(stage_one, [orbitals.shape, (planes + 4, rows, lanes)], slab, *both_sides(slab))
    total = bands * orbs
    u, send, half_diag = call(
        stage_two,
        [orbitals.shape, (bands, lanes // bands + 2, orbs // 2, 2 * planes * rows), (lanes, 2 * planes * rows)],
        g,
        *both_sides(g),
        slab,
        diag,
    )
    got = lax.all_to_all(send, "y", 0, 0, tiled=True)
    (edge,) = call(pack_edge, [(lanes // bands // 2, bands, orbs // 2, 2 * planes * rows)], got)
    edge = lax.ppermute(edge, GRID, down)
    over, half = call(gram_own, [(total, total)] * 2, got, half_diag, flops=1 << 30)
    (part,) = call(gram_edge, [(bands, 2, orbs, total)], got, edge, over, half)

    first = ("y", "x", "core")
    pieces = lax.axis_size(first)
    flat = part.reshape(pieces, -1, bands * orbs)
    mine = lax.all_to_all(flat, first, 0, 0, tiled=True).sum(0)
    spread = jnp.broadcast_to(mine[None], (slabs, *mine.shape))
    back = lax.all_to_all(spread, GRID, 0, 0, tiled=True)
    nx, nz, nc = (lax.axis_size(a) for a in GRID)
    both = back.reshape(nx, nz, nc, *mine.shape).sum(1) / cells_all
    both = both.reshape(2, orbs, bands * orbs)
    return u, both[0], both[1]


def solution(mesh):
    devices = mesh.devices.reshape(4, 8, 2, 8)
    fine = Mesh(devices, ("x", "z", "core", "y"))
    in_specs = (P("y", GRID, None, None), P(GRID, None, None))
    out_specs = (P("y", GRID, None, None), P("y", None), P("y", None))
    return jax.shard_map(per_device, mesh=fine, in_specs=in_specs, out_specs=out_specs, check_vma=False)
```

```python
import jax
import jax.numpy as jnp
from jax import lax
from jax.experimental import pallas as pl
from jax.experimental.pallas import tpu as pltpu
from jax.sharding import Mesh, PartitionSpec as P

SHIFT_MID = 6.5
HALF_WIDTH = 3.5
DIAG = 3.0 * 30.0 / 24.0
NEAR = -16.0 / 24.0
FAR = 1.0 / 24.0
GRID = ("x", "z", "core")
SIDE = 4
VMEM = pl.BlockSpec(memory_space=pltpu.VMEM)
LIMIT = pltpu.CompilerParams(vmem_limit_bytes=24 * 1024 * 1024)


def ring_shift(size, by):
    return [(i, (i + by) % size) for i in range(size)]


def scaled_op(padded, diag):
    mid = padded[2:-2]
    rows, lanes = mid.shape[1], mid.shape[2]
    near = padded[1:-3] + padded[3:-1]
    far = padded[:-4] + padded[4:]
    near = near + (pltpu.roll(mid, 1, 1) + pltpu.roll(mid, rows - 1, 1))
    far = far + (pltpu.roll(mid, 2, 1) + pltpu.roll(mid, rows - 2, 1))
    near = near + (pltpu.roll(mid, 1, 2) + pltpu.roll(mid, lanes - 1, 2))
    far = far + (pltpu.roll(mid, 2, 2) + pltpu.roll(mid, lanes - 2, 2))
    return diag * mid + (NEAR / HALF_WIDTH) * near + (FAR / HALF_WIDTH) * far


def by_core(run, on, off):
    core = lax.axis_index("core")
    pl.when(core == 0)(lambda: run(off, on))
    pl.when(core == 1)(lambda: run(on, off))


def stage_one(own, on, off, out, diag):
    orbs = own.shape[0] - 1

    def run(lo, hi):
        v = jnp.concatenate([lo[orbs, 2:], own[orbs], hi[orbs, :2]], axis=0)
        diag[...] = (v + (DIAG - SHIFT_MID)) / HALF_WIDTH

        def step(group, carry):
            members = [group * SIDE + i for i in range(SIDE)]
            firsts = [scaled_op(jnp.concatenate([lo[o], own[o], hi[o]], axis=0), diag[...]) for o in members]
            for o, first in zip(members, firsts):
                out[o] = 2.0 * scaled_op(first, diag[2:-2]) - own[o]
            return carry

        lax.fori_loop(0, orbs // SIDE, step, 0)

    by_core(run, on, off)


def stage_two(gown, on, off, fown, diag, out, send, half_diag):
    orbs, planes, rows, lanes = gown.shape
    peers, depth, octet, _ = send.shape
    chunk = lanes // peers
    half = 0.5 * (HALF_WIDTH * diag[2:-2] + SHIFT_MID)
    half_diag[...] = jnp.concatenate([half.reshape(planes * rows, lanes)] * 2, axis=0).T

    def run(lo, hi):
        def step(group, carry):
            octets = [group * (SIDE // 2) + i for i in range(SIDE // 2)]
            members = [o for p in octets for o in (p, p + octet)]
            firsts = [scaled_op(jnp.concatenate([lo[o], gown[o], hi[o]], axis=0), diag[...]) for o in members]
            us = []
            for o, first in zip(members, firsts):
                u = 4.0 * scaled_op(first, diag[2:-2]) - 2.0 * gown[o] - fown[o]
                out[o] = u
                us.append(u.reshape(planes * rows, lanes))
            for i, p in enumerate(octets):
                lines = jnp.concatenate(us[2 * i : 2 * i + 2], axis=0).T
                for k in range(peers):
                    at = (k + 1) % peers * chunk
                    send[k, :chunk, pl.ds(p, 1), :] = lines[k * chunk : (k + 1) * chunk][:, None, :]
                    send[k, chunk:, pl.ds(p, 1), :] = lines[at : at + depth - chunk][:, None, :]
            return carry

        lax.fori_loop(0, 2 * octet // SIDE, step, 0)

    by_core(run, on, off)


def lane_ids(like):
    return lax.broadcasted_iota(jnp.int32, like.shape, 2)


def pack_edge(got, out):
    for j in range(out.shape[0]):
        a, b = got[:, 2 * j], got[:, 2 * j + 1]
        out[j] = jnp.where(lane_ids(a) % 64 < 32, pltpu.roll(a, 96, 2), b)


def split(x):
    high = x.astype(jnp.bfloat16)
    return high, (x - high.astype(jnp.float32)).astype(jnp.bfloat16)


def dot3(a, b):
    dims = (((1,), (1,)), ((), ()))
    (ah, al), (bh, bl) = a, b
    parts = [
        lax.dot_general(x, y, dims, preferred_element_type=jnp.float32) for x, y in ((ah, bh), (ah, bl), (al, bh))
    ]
    return parts[0] + (parts[1] + parts[2])


def orbital_rows(a, b):
    low = lane_ids(a) < 64
    top = jnp.where(low, a, pltpu.roll(b, 64, 2))
    end = jnp.where(low, pltpu.roll(a, 64, 2), b)
    return jnp.stack([top, end], axis=1).reshape(-1, a.shape[-1])


def gram_own(got, half_diag, over, half, first):
    bands, depth, octet, _ = got.shape
    start = pl.multiple_of(lax.axis_index("y") * (depth - 2), 16)
    lane = lane_ids(got[:, 0])
    x = lane % 16
    z = lane % 64 // 16

    def one_sided(y):
        u = got[:, y]
        near = got[:, y + 1] + jnp.where(x < 15, pltpu.roll(u, 127, 2), pltpu.roll(u, 15, 2))
        far = got[:, y + 2] + jnp.where(x < 14, pltpu.roll(u, 126, 2), pltpu.roll(u, 14, 2))
        near = near + jnp.where(z >= 1, pltpu.roll(u, 16, 2), 0.0)
        far = far + jnp.where(z >= 2, pltpu.roll(u, 32, 2), 0.0)
        return half_diag[pl.ds(start + y, 1), :][None] * u + NEAR * near + FAR * far

    total_over, total_half = 0.0, 0.0
    for y in range(0, depth - 2, 2):
        u = split(orbital_rows(got[:, y], got[:, y + 1]))
        w = split(orbital_rows(one_sided(y), one_sided(y + 1)))
        total_over = total_over + dot3(u, u)
        total_half = total_half + dot3(u, w)
    over[...] = total_over
    half[...] = total_half
    for j in range(first.shape[0]):
        two = []
        for y in (4 * j, 4 * j + 2):
            two.append(jnp.where(lane % 64 < 32, got[:, y], pltpu.roll(got[:, y + 1], 32, 2)))
        first[j] = orbital_rows(*two)


def gram_edge(edge, first, over, half, out):
    bands = edge.shape[1]
    third = lane_ids(edge[0]) % 32 < 16
    total = half[...]
    for j in range(first.shape[0]):
        two = []
        for e in (edge[2 * j], edge[2 * j + 1]):
            two.append(FAR * e + jnp.where(third, NEAR * pltpu.roll(e, 112, 2), 0.0))
        total = total + dot3(split(first[j]), split(orbital_rows(*two)))
    out[:, 0] = over[...].reshape(bands, -1, total.shape[-1])
    out[:, 1] = (total + total.T).reshape(bands, -1, total.shape[-1])


def call(body, out_shapes, *args, flops=0):
    return pl.pallas_call(
        body,
        out_shape=[jax.ShapeDtypeStruct(s, jnp.float32) for s in out_shapes],
        in_specs=[VMEM] * len(args),
        out_specs=[VMEM] * len(out_shapes),
        compiler_params=LIMIT,
        cost_estimate=pl.CostEstimate(flops=flops, bytes_accessed=1 << 20, transcendentals=0),
    )(*args)


def per_device(orbitals, potential):
    orbs, planes, rows, lanes = orbitals.shape
    slabs = lax.axis_size(GRID)
    bands = lax.axis_size("y")
    cells_all = slabs * planes * rows * lanes
    following = ring_shift(slabs, 1)
    outer = [(i, (i + (1 if i % 2 else -1)) % slabs) for i in range(slabs)]

    def both_sides(slab):
        off = lax.ppermute(slab, GRID, outer)
        return lax.ppermute(slab, "core", [(0, 1), (1, 0)]), off

    slab = jnp.concatenate([orbitals, potential[None]], axis=0)
    g, diag = call(stage_one, [orbitals.shape, (planes + 4, rows, lanes)], slab, *both_sides(slab))
    total = bands * orbs
    u, send, half_diag = call(
        stage_two,
        [orbitals.shape, (bands, lanes // bands + 2, orbs // 2, 2 * planes * rows), (lanes, 2 * planes * rows)],
        g,
        *both_sides(g),
        slab,
        diag,
    )
    got = lax.all_to_all(send, "y", 0, 0, tiled=True)
    (edge,) = call(pack_edge, [(lanes // bands // 2, bands, orbs // 2, 2 * planes * rows)], got)
    edge = lax.ppermute(edge, GRID, following)
    firsts = (lanes // bands // 4, total, 2 * planes * rows)
    over, half, first = call(gram_own, [(total, total), (total, total), firsts], got, half_diag, flops=1 << 30)
    (part,) = call(gram_edge, [(bands, 2, orbs, total)], edge, first, over, half)

    reducers = ("y", "x", "core")
    pieces = lax.axis_size(reducers)
    flat = part.reshape(pieces, -1, bands * orbs)
    mine = lax.all_to_all(flat, reducers, 0, 0, tiled=True).sum(0)
    spread = jnp.broadcast_to(mine[None], (slabs, *mine.shape))
    back = lax.all_to_all(spread, GRID, 0, 0, tiled=True)
    nx, nz, nc = (lax.axis_size(a) for a in GRID)
    both = back.reshape(nx, nz, nc, *mine.shape).sum(1) / cells_all
    both = both.reshape(2, orbs, bands * orbs)
    return u, both[0], both[1]


def solution(mesh):
    devices = mesh.devices.reshape(4, 8, 2, 8)
    fine = Mesh(devices, ("x", "z", "core", "y"))
    in_specs = (P("y", GRID, None, None), P(GRID, None, None))
    out_specs = (P("y", GRID, None, None), P("y", None), P("y", None))
    return jax.shard_map(per_device, mesh=fine, in_specs=in_specs, out_specs=out_specs, check_vma=False)
```

```python
import jax
import jax.numpy as jnp
from jax import lax
from jax.experimental import pallas as pl
from jax.experimental.pallas import tpu as pltpu
from jax.sharding import Mesh, PartitionSpec as P

SHIFT_MID = 6.5
HALF_WIDTH = 3.5
DIAG = 3.0 * 30.0 / 24.0
NEAR = -16.0 / 24.0
FAR = 1.0 / 24.0
GRID = ("x", "z", "core")
REDUCERS = ("y", "x")
SIDE = 8
VMEM = pl.BlockSpec(memory_space=pltpu.VMEM)
LIMIT = pltpu.CompilerParams(vmem_limit_bytes=24 * 1024 * 1024)


def ring_shift(size, by):
    return [(i, (i + by) % size) for i in range(size)]


def scaled_op(padded, diag):
    mid = padded[2:-2]
    rows, lanes = mid.shape[1], mid.shape[2]
    near = padded[1:-3] + padded[3:-1]
    far = padded[:-4] + padded[4:]
    near = near + (pltpu.roll(mid, 1, 1) + pltpu.roll(mid, rows - 1, 1))
    far = far + (pltpu.roll(mid, 2, 1) + pltpu.roll(mid, rows - 2, 1))
    near = near + (pltpu.roll(mid, 1, 2) + pltpu.roll(mid, lanes - 1, 2))
    far = far + (pltpu.roll(mid, 2, 2) + pltpu.roll(mid, lanes - 2, 2))
    return diag * mid + (NEAR / HALF_WIDTH) * near + (FAR / HALF_WIDTH) * far


def by_core(run, on, off):
    core = lax.axis_index("core")
    pl.when(core == 0)(lambda: run(off, on))
    pl.when(core == 1)(lambda: run(on, off))


def stage_one(own, on, off, out, diag):
    orbs = own.shape[0] - 1

    def run(lo, hi):
        v = jnp.concatenate([lo[orbs, 2:], own[orbs], hi[orbs, :2]], axis=0)
        diag[...] = (v + (DIAG - SHIFT_MID)) / HALF_WIDTH

        def step(group, carry):
            members = [group * SIDE + i for i in range(SIDE)]
            firsts = [scaled_op(jnp.concatenate([lo[o], own[o], hi[o]], axis=0), diag[...]) for o in members]
            for o, first in zip(members, firsts):
                out[o] = 2.0 * scaled_op(first, diag[2:-2]) - own[o]
            return carry

        lax.fori_loop(0, orbs // SIDE, step, 0)

    by_core(run, on, off)


def stage_two(gown, on, off, fown, diag, out, send, half_diag):
    orbs, planes, rows, lanes = gown.shape
    peers, depth, octet, _ = send.shape
    chunk = lanes // peers
    half = 0.5 * (HALF_WIDTH * diag[2:-2] + SHIFT_MID)
    half_diag[...] = jnp.concatenate([half.reshape(planes * rows, lanes)] * 2, axis=0).T

    def run(lo, hi):
        def step(group, carry):
            octets = [group * (SIDE // 2) + i for i in range(SIDE // 2)]
            members = [o for p in octets for o in (p, p + octet)]
            firsts = [scaled_op(jnp.concatenate([lo[o], gown[o], hi[o]], axis=0), diag[...]) for o in members]
            us = []
            for o, first in zip(members, firsts):
                u = 4.0 * scaled_op(first, diag[2:-2]) - 2.0 * gown[o] - fown[o]
                out[o] = u
                us.append(u.reshape(planes * rows, lanes))
            for i, p in enumerate(octets):
                lines = jnp.concatenate(us[2 * i : 2 * i + 2], axis=0).T
                for k in range(peers):
                    at = (k + 1) % peers * chunk
                    send[k, :chunk, pl.ds(p, 1), :] = lines[k * chunk : (k + 1) * chunk][:, None, :]
                    send[k, chunk:, pl.ds(p, 1), :] = lines[at : at + depth - chunk][:, None, :]
            return carry

        lax.fori_loop(0, 2 * octet // SIDE, step, 0)

    by_core(run, on, off)


def lane_ids(like):
    return lax.broadcasted_iota(jnp.int32, like.shape, 2)


def pack_edge(got, out):
    for j in range(out.shape[0]):
        a, b = got[:, 2 * j], got[:, 2 * j + 1]
        out[j] = jnp.where(lane_ids(a) % 64 < 32, pltpu.roll(a, 96, 2), b)


def split(x):
    high = x.astype(jnp.bfloat16)
    return high, (x - high.astype(jnp.float32)).astype(jnp.bfloat16)


def dot3(a, b):
    dims = (((1,), (1,)), ((), ()))
    (ah, al), (bh, bl) = a, b
    parts = [
        lax.dot_general(x, y, dims, preferred_element_type=jnp.float32) for x, y in ((ah, bh), (ah, bl), (al, bh))
    ]
    return parts[0] + (parts[1] + parts[2])


def orbital_rows(a, b):
    low = lane_ids(a) < 64
    top = jnp.where(low, a, pltpu.roll(b, 64, 2))
    end = jnp.where(low, pltpu.roll(a, 64, 2), b)
    return jnp.stack([top, end], axis=1).reshape(-1, a.shape[-1])


def gram_own(got, half_diag, u, over, half, first, kept, done):
    keep = pltpu.make_async_copy(u, kept, done)
    keep.start()
    bands, depth, octet, _ = got.shape
    start = pl.multiple_of(lax.axis_index("y") * (depth - 2), 16)
    lane = lane_ids(got[:, 0])
    x = lane % 16
    z = lane % 64 // 16

    def one_sided(y):
        u = got[:, y]
        near = got[:, y + 1] + jnp.where(x < 15, pltpu.roll(u, 127, 2), pltpu.roll(u, 15, 2))
        far = got[:, y + 2] + jnp.where(x < 14, pltpu.roll(u, 126, 2), pltpu.roll(u, 14, 2))
        near = near + jnp.where(z >= 1, pltpu.roll(u, 16, 2), 0.0)
        far = far + jnp.where(z >= 2, pltpu.roll(u, 32, 2), 0.0)
        return half_diag[pl.ds(start + y, 1), :][None] * u + NEAR * near + FAR * far

    total_over, total_half = 0.0, 0.0
    for y in range(0, depth - 2, 2):
        u = split(orbital_rows(got[:, y], got[:, y + 1]))
        w = split(orbital_rows(one_sided(y), one_sided(y + 1)))
        total_over = total_over + dot3(u, u)
        total_half = total_half + dot3(u, w)
    over[...] = total_over
    half[...] = total_half
    for j in range(first.shape[0]):
        two = []
        for y in (4 * j, 4 * j + 2):
            two.append(jnp.where(lane % 64 < 32, got[:, y], pltpu.roll(got[:, y + 1], 32, 2)))
        first[j] = orbital_rows(*two)
    keep.wait()


def gram_edge(edge, first, over, half, out):
    bands = edge.shape[1]
    third = lane_ids(edge[0]) % 32 < 16
    total = half[...]
    for j in range(first.shape[0]):
        two = []
        for e in (edge[2 * j], edge[2 * j + 1]):
            two.append(FAR * e + jnp.where(third, NEAR * pltpu.roll(e, 112, 2), 0.0))
        total = total + dot3(split(first[j]), split(orbital_rows(*two)))
    out[:, 0] = over[...].reshape(bands, -1, total.shape[-1])
    out[:, 1] = (total + total.T).reshape(bands, -1, total.shape[-1])


def call(body, out_shapes, *args, kept=0, scratch=(), flops=0):
    places = [VMEM] * (len(out_shapes) - kept) + [pl.BlockSpec(memory_space=pl.ANY)] * kept
    return pl.pallas_call(
        body,
        out_shape=[jax.ShapeDtypeStruct(s, jnp.float32) for s in out_shapes],
        in_specs=[VMEM] * len(args),
        out_specs=places,
        scratch_shapes=scratch,
        compiler_params=LIMIT,
        cost_estimate=pl.CostEstimate(flops=flops, bytes_accessed=1 << 20, transcendentals=0),
    )(*args)


def per_device(orbitals, potential):
    orbs, planes, rows, lanes = orbitals.shape
    slabs = lax.axis_size(GRID)
    bands = lax.axis_size("y")
    cells_all = slabs * planes * rows * lanes
    following = ring_shift(slabs, 1)
    outer = [(i, (i + (1 if i % 2 else -1)) % slabs) for i in range(slabs)]

    def both_sides(slab):
        off = lax.ppermute(slab, GRID, outer)
        return lax.ppermute(slab, "core", [(0, 1), (1, 0)]), off

    slab = jnp.concatenate([orbitals, potential[None]], axis=0)
    g, diag = call(stage_one, [orbitals.shape, (planes + 4, rows, lanes)], slab, *both_sides(slab))
    total = bands * orbs
    u, send, half_diag = call(
        stage_two,
        [orbitals.shape, (bands, lanes // bands + 2, orbs // 2, 2 * planes * rows), (lanes, 2 * planes * rows)],
        g,
        *both_sides(g),
        slab,
        diag,
    )
    got = lax.all_to_all(send, "y", 0, 0, tiled=True)
    (edge,) = call(pack_edge, [(lanes // bands // 2, bands, orbs // 2, 2 * planes * rows)], got)
    edge = lax.ppermute(edge, GRID, following)
    firsts = (lanes // bands // 4, total, 2 * planes * rows)
    over, half, first, u = call(
        gram_own,
        [(total, total), (total, total), firsts, u.shape],
        got,
        half_diag,
        u,
        kept=1,
        scratch=[pltpu.SemaphoreType.DMA],
        flops=1 << 30,
    )
    (part,) = call(gram_edge, [(bands, 2, orbs, total)], edge, first, over, half)

    pieces = lax.axis_size(REDUCERS)
    flat = part.reshape(pieces, -1, bands * orbs)
    mine = lax.all_to_all(flat, REDUCERS, 0, 0, tiled=True).sum(0)
    mine = lax.psum(mine, "core")
    spread = jnp.broadcast_to(mine[None], (slabs // 2, *mine.shape))
    back = lax.all_to_all(spread, ("x", "z"), 0, 0, tiled=True)
    both = back.reshape(lax.axis_size("x"), lax.axis_size("z"), *mine.shape).sum(1) / cells_all
    both = both.reshape(2, orbs, bands * orbs)
    return u, both[0], both[1]


def solution(mesh):
    devices = mesh.devices.reshape(4, 8, 2, 8)
    fine = Mesh(devices, ("x", "z", "core", "y"))
    in_specs = (P("y", GRID, None, None), P(GRID, None, None))
    out_specs = (P("y", GRID, None, None), P("y", None), P("y", None))
    return jax.shard_map(per_device, mesh=fine, in_specs=in_specs, out_specs=out_specs, check_vma=False)
```

```python
import jax
import jax.numpy as jnp
from jax import lax
from jax.experimental import pallas as pl
from jax.experimental.pallas import tpu as pltpu
from jax.sharding import Mesh, PartitionSpec as P

SHIFT_MID = 6.5
HALF_WIDTH = 3.5
DIAG = 3.0 * 30.0 / 24.0
NEAR = -16.0 / 24.0
FAR = 1.0 / 24.0
GRID = ("x", "z", "core")
REDUCERS = ("y", "x")
SIDE = 8
VMEM = pl.BlockSpec(memory_space=pltpu.VMEM)
LIMIT = pltpu.CompilerParams(vmem_limit_bytes=24 * 1024 * 1024)


def ring_shift(size, by):
    return [(i, (i + by) % size) for i in range(size)]


def scaled_xy(mid, diag):
    rows, lanes = mid.shape[1], mid.shape[2]
    near = pltpu.roll(mid, 1, 1) + pltpu.roll(mid, rows - 1, 1)
    far = pltpu.roll(mid, 2, 1) + pltpu.roll(mid, rows - 2, 1)
    near = near + (pltpu.roll(mid, 1, 2) + pltpu.roll(mid, lanes - 1, 2))
    far = far + (pltpu.roll(mid, 2, 2) + pltpu.roll(mid, lanes - 2, 2))
    return diag * mid + (NEAR / HALF_WIDTH) * near + (FAR / HALF_WIDTH) * far


def scaled_z(padded):
    near = padded[1:-3] + padded[3:-1]
    far = padded[:-4] + padded[4:]
    return (NEAR / HALF_WIDTH) * near + (FAR / HALF_WIDTH) * far


def scaled_op(padded, diag):
    return scaled_xy(padded[2:-2], diag) + scaled_z(padded)


def scaled_pot(v):
    return (v + (DIAG - SHIFT_MID)) / HALF_WIDTH


def ahead(own, diag, own_xy):
    orbs = own_xy.shape[0]

    def step(group, carry):
        for o in [group * SIDE + i for i in range(SIDE)]:
            own_xy[o] = scaled_xy(own[o], diag)
        return carry

    lax.fori_loop(0, orbs // SIDE, step, 0)


def ahead_one(own, own_xy):
    ahead(own, scaled_pot(own[own_xy.shape[0]]), own_xy)


def ahead_two(own, diag, own_xy, half_diag):
    _, planes, rows, lanes = own.shape
    half = 0.5 * (HALF_WIDTH * diag[2:-2] + SHIFT_MID)
    half_diag[...] = jnp.concatenate([half.reshape(planes * rows, lanes)] * 2, axis=0).T
    ahead(own, diag[2:-2], own_xy)


def by_core(run, on, off):
    core = lax.axis_index("core")
    pl.when(core == 0)(lambda: run(off, on))
    pl.when(core == 1)(lambda: run(on, off))


def first_op(lo, own, hi, own_xy, diag, o):
    before, after = scaled_xy(lo[o, 2:], diag[:2]), scaled_xy(hi[o, :2], diag[-2:])
    return jnp.concatenate([before, own_xy[o], after], axis=0) + scaled_z(
        jnp.concatenate([lo[o], own[o], hi[o]], axis=0)
    )


def stage_one(own, on, off, own_xy, out, diag):
    orbs = own.shape[0] - 1

    def run(lo, hi):
        diag[...] = scaled_pot(jnp.concatenate([lo[orbs, 2:], own[orbs], hi[orbs, :2]], axis=0))

        def step(group, carry):
            members = [group * SIDE + i for i in range(SIDE)]
            firsts = [first_op(lo, own, hi, own_xy, diag[...], o) for o in members]
            for o, first in zip(members, firsts):
                out[o] = 2.0 * scaled_op(first, diag[2:-2]) - own[o]
            return carry

        lax.fori_loop(0, orbs // SIDE, step, 0)

    by_core(run, on, off)


def stage_two(gown, on, off, own_xy, fown, diag, out, send):
    orbs, planes, rows, lanes = gown.shape
    peers, depth, octet, _ = send.shape
    chunk = lanes // peers

    def run(lo, hi):
        def step(group, carry):
            octets = [group * (SIDE // 2) + i for i in range(SIDE // 2)]
            members = [o for p in octets for o in (p, p + octet)]
            firsts = [first_op(lo, gown, hi, own_xy, diag[...], o) for o in members]
            us = []
            for o, first in zip(members, firsts):
                u = 4.0 * scaled_op(first, diag[2:-2]) - 2.0 * gown[o] - fown[o]
                out[o] = u
                us.append(u.reshape(planes * rows, lanes))
            for i, p in enumerate(octets):
                lines = jnp.concatenate(us[2 * i : 2 * i + 2], axis=0).T
                for k in range(peers):
                    at = (k + 1) % peers * chunk
                    send[k, :chunk, pl.ds(p, 1), :] = lines[k * chunk : (k + 1) * chunk][:, None, :]
                    send[k, chunk:, pl.ds(p, 1), :] = lines[at : at + depth - chunk][:, None, :]
            return carry

        lax.fori_loop(0, 2 * octet // SIDE, step, 0)

    by_core(run, on, off)


def lane_ids(like):
    return lax.broadcasted_iota(jnp.int32, like.shape, 2)


def pack_edge(got, out):
    for j in range(out.shape[0]):
        a, b = got[:, 2 * j], got[:, 2 * j + 1]
        out[j] = jnp.where(lane_ids(a) % 64 < 32, pltpu.roll(a, 96, 2), b)


def split(x):
    high = x.astype(jnp.bfloat16)
    return high, (x - high.astype(jnp.float32)).astype(jnp.bfloat16)


def dot3(a, b):
    dims = (((1,), (1,)), ((), ()))
    (ah, al), (bh, bl) = a, b
    parts = [
        lax.dot_general(x, y, dims, preferred_element_type=jnp.float32) for x, y in ((ah, bh), (ah, bl), (al, bh))
    ]
    return parts[0] + (parts[1] + parts[2])


def orbital_rows(a, b):
    low = lane_ids(a) < 64
    top = jnp.where(low, a, pltpu.roll(b, 64, 2))
    end = jnp.where(low, pltpu.roll(a, 64, 2), b)
    return jnp.stack([top, end], axis=1).reshape(-1, a.shape[-1])


def gram_own(got, half_diag, u, over, half, first, kept, done):
    keep = pltpu.make_async_copy(u, kept, done)
    keep.start()
    bands, depth, octet, _ = got.shape
    start = pl.multiple_of(lax.axis_index("y") * (depth - 2), 16)
    lane = lane_ids(got[:, 0])
    x = lane % 16
    z = lane % 64 // 16

    def one_sided(y):
        u = got[:, y]
        near = got[:, y + 1] + jnp.where(x < 15, pltpu.roll(u, 127, 2), pltpu.roll(u, 15, 2))
        far = got[:, y + 2] + jnp.where(x < 14, pltpu.roll(u, 126, 2), pltpu.roll(u, 14, 2))
        near = near + jnp.where(z >= 1, pltpu.roll(u, 16, 2), 0.0)
        far = far + jnp.where(z >= 2, pltpu.roll(u, 32, 2), 0.0)
        return half_diag[pl.ds(start + y, 1), :][None] * u + NEAR * near + FAR * far

    total_over, total_half = 0.0, 0.0
    for y in range(0, depth - 2, 2):
        u = split(orbital_rows(got[:, y], got[:, y + 1]))
        w = split(orbital_rows(one_sided(y), one_sided(y + 1)))
        total_over = total_over + dot3(u, u)
        total_half = total_half + dot3(u, w)
    over[...] = total_over
    half[...] = total_half
    for j in range(first.shape[0]):
        two = []
        for y in (4 * j, 4 * j + 2):
            two.append(jnp.where(lane % 64 < 32, got[:, y], pltpu.roll(got[:, y + 1], 32, 2)))
        first[j] = orbital_rows(*two)
    keep.wait()


def gram_edge(edge, first, over, half, out):
    bands = edge.shape[1]
    third = lane_ids(edge[0]) % 32 < 16
    total = half[...]
    for j in range(first.shape[0]):
        two = []
        for e in (edge[2 * j], edge[2 * j + 1]):
            two.append(FAR * e + jnp.where(third, NEAR * pltpu.roll(e, 112, 2), 0.0))
        total = total + dot3(split(first[j]), split(orbital_rows(*two)))
    out[:, 0] = over[...].reshape(bands, -1, total.shape[-1])
    out[:, 1] = (total + total.T).reshape(bands, -1, total.shape[-1])


def call(body, out_shapes, *args, kept=0, scratch=(), flops=0):
    places = [VMEM] * (len(out_shapes) - kept) + [pl.BlockSpec(memory_space=pl.ANY)] * kept
    return pl.pallas_call(
        body,
        out_shape=[jax.ShapeDtypeStruct(s, jnp.float32) for s in out_shapes],
        in_specs=[VMEM] * len(args),
        out_specs=places,
        scratch_shapes=scratch,
        compiler_params=LIMIT,
        cost_estimate=pl.CostEstimate(flops=flops, bytes_accessed=1 << 20, transcendentals=0),
    )(*args)


def per_device(orbitals, potential):
    orbs, planes, rows, lanes = orbitals.shape
    slabs = lax.axis_size(GRID)
    bands = lax.axis_size("y")
    cells_all = slabs * planes * rows * lanes
    following = ring_shift(slabs, 1)
    outer = [(i, (i + (1 if i % 2 else -1)) % slabs) for i in range(slabs)]

    def both_sides(slab):
        off = lax.ppermute(slab, GRID, outer)
        return lax.ppermute(slab, "core", [(0, 1), (1, 0)]), off

    slab = jnp.concatenate([orbitals, potential[None]], axis=0)
    on, off = both_sides(slab)
    (own_xy,) = call(ahead_one, [orbitals.shape], slab, flops=1 << 28)
    g, diag = call(stage_one, [orbitals.shape, (planes + 4, rows, lanes)], slab, on, off, own_xy)
    on, off = both_sides(g)
    own_xy, half_diag = call(ahead_two, [orbitals.shape, (lanes, 2 * planes * rows)], g, diag, flops=1 << 28)
    total = bands * orbs
    u, send = call(
        stage_two,
        [orbitals.shape, (bands, lanes // bands + 2, orbs // 2, 2 * planes * rows)],
        g,
        on,
        off,
        own_xy,
        slab,
        diag,
    )
    got = lax.all_to_all(send, "y", 0, 0, tiled=True)
    (edge,) = call(pack_edge, [(lanes // bands // 2, bands, orbs // 2, 2 * planes * rows)], got)
    edge = lax.ppermute(edge, GRID, following)
    firsts = (lanes // bands // 4, total, 2 * planes * rows)
    over, half, first, u = call(
        gram_own,
        [(total, total), (total, total), firsts, u.shape],
        got,
        half_diag,
        u,
        kept=1,
        scratch=[pltpu.SemaphoreType.DMA],
        flops=1 << 30,
    )
    (part,) = call(gram_edge, [(bands, 2, orbs, total)], edge, first, over, half)

    pieces = lax.axis_size(REDUCERS)
    flat = part.reshape(pieces, -1, bands * orbs)
    mine = lax.all_to_all(flat, REDUCERS, 0, 0, tiled=True).sum(0)
    mine = lax.psum(mine, "core")
    spread = jnp.broadcast_to(mine[None], (slabs // 2, *mine.shape))
    back = lax.all_to_all(spread, ("x", "z"), 0, 0, tiled=True)
    both = back.reshape(lax.axis_size("x"), lax.axis_size("z"), *mine.shape).sum(1) / cells_all
    both = both.reshape(2, orbs, bands * orbs)
    return u, both[0], both[1]


def solution(mesh):
    devices = mesh.devices.reshape(4, 8, 2, 8)
    fine = Mesh(devices, ("x", "z", "core", "y"))
    in_specs = (P("y", GRID, None, None), P(GRID, None, None))
    out_specs = (P("y", GRID, None, None), P("y", None), P("y", None))
    return jax.shard_map(per_device, mesh=fine, in_specs=in_specs, out_specs=out_specs, check_vma=False)
```

```python
import jax
import jax.numpy as jnp
from jax import lax
from jax.experimental import pallas as pl
from jax.experimental.pallas import tpu as pltpu
from jax.sharding import Mesh, PartitionSpec as P

SHIFT_MID = 6.5
HALF_WIDTH = 3.5
DIAG = 3.0 * 30.0 / 24.0
NEAR = -16.0 / 24.0
FAR = 1.0 / 24.0
GRID = ("x", "z", "core")
REDUCERS = ("y", "x")
SIDE = 8
VMEM = pl.BlockSpec(memory_space=pltpu.VMEM)
LIMIT = pltpu.CompilerParams(vmem_limit_bytes=24 * 1024 * 1024)


def ring_shift(size, by):
    return [(i, (i + by) % size) for i in range(size)]


def scaled_xy(mid, diag):
    rows, lanes = mid.shape[1], mid.shape[2]
    near = pltpu.roll(mid, 1, 1) + pltpu.roll(mid, rows - 1, 1)
    far = pltpu.roll(mid, 2, 1) + pltpu.roll(mid, rows - 2, 1)
    near = near + (pltpu.roll(mid, 1, 2) + pltpu.roll(mid, lanes - 1, 2))
    far = far + (pltpu.roll(mid, 2, 2) + pltpu.roll(mid, lanes - 2, 2))
    return diag * mid + (NEAR / HALF_WIDTH) * near + (FAR / HALF_WIDTH) * far


def scaled_z(padded):
    near = padded[1:-3] + padded[3:-1]
    far = padded[:-4] + padded[4:]
    return (NEAR / HALF_WIDTH) * near + (FAR / HALF_WIDTH) * far


def scaled_op(padded, diag):
    return scaled_xy(padded[2:-2], diag) + scaled_z(padded)


def scaled_pot(v):
    return (v + (DIAG - SHIFT_MID)) / HALF_WIDTH


def ahead(own, diag, own_xy):
    orbs = own_xy.shape[0]

    def step(group, carry):
        for o in [group * SIDE + i for i in range(SIDE)]:
            own_xy[o] = scaled_xy(own[o], diag)
        return carry

    lax.fori_loop(0, orbs // SIDE, step, 0)


def ahead_one(own, own_xy):
    ahead(own, scaled_pot(own[own_xy.shape[0]]), own_xy)


def ahead_two(own, diag, own_xy, half_diag):
    _, planes, rows, lanes = own.shape
    half = 0.5 * (HALF_WIDTH * diag[2:-2] + SHIFT_MID)
    half_diag[...] = jnp.concatenate([half.reshape(planes * rows, lanes)] * 2, axis=0).T
    ahead(own, diag[2:-2], own_xy)


def by_core(run, on, off):
    core = lax.axis_index("core")
    pl.when(core == 0)(lambda: run(off, on))
    pl.when(core == 1)(lambda: run(on, off))


def first_op(lo, own, hi, own_xy, diag, o):
    before, after = scaled_xy(lo[o, 2:], diag[:2]), scaled_xy(hi[o, :2], diag[-2:])
    return jnp.concatenate([before, own_xy[o], after], axis=0) + scaled_z(
        jnp.concatenate([lo[o], own[o], hi[o]], axis=0)
    )


def stage_one(own, on, off, own_xy, out, diag):
    orbs = own.shape[0] - 1

    def run(lo, hi):
        diag[...] = scaled_pot(jnp.concatenate([lo[orbs, 2:], own[orbs], hi[orbs, :2]], axis=0))

        def step(group, carry):
            members = [group * SIDE + i for i in range(SIDE)]
            firsts = [first_op(lo, own, hi, own_xy, diag[...], o) for o in members]
            for o, first in zip(members, firsts):
                out[o] = 2.0 * scaled_op(first, diag[2:-2]) - own[o]
            return carry

        lax.fori_loop(0, orbs // SIDE, step, 0)

    by_core(run, on, off)


def stage_two(gown, on, off, own_xy, fown, diag, out, send):
    orbs, planes, rows, lanes = gown.shape
    peers, chunk, octet, _ = send.shape

    def run(lo, hi):
        def step(group, carry):
            octets = [group * (SIDE // 2) + i for i in range(SIDE // 2)]
            members = [o for p in octets for o in (p, p + octet)]
            firsts = [first_op(lo, gown, hi, own_xy, diag[...], o) for o in members]
            us = []
            for o, first in zip(members, firsts):
                u = 4.0 * scaled_op(first, diag[2:-2]) - 2.0 * gown[o] - fown[o]
                out[o] = u
                us.append(u.reshape(planes * rows, lanes))
            for i, p in enumerate(octets):
                lines = jnp.concatenate(us[2 * i : 2 * i + 2], axis=0).T
                for k in range(peers):
                    send[k, :, pl.ds(p, 1), :] = lines[k * chunk : (k + 1) * chunk][:, None, :]
            return carry

        lax.fori_loop(0, 2 * octet // SIDE, step, 0)

    by_core(run, on, off)


def lane_ids(like):
    return lax.broadcasted_iota(jnp.int32, like.shape, 2)


def pack_edge(got, out, head):
    head[...] = got[:, :2]
    for j in range(out.shape[0]):
        a, b = got[:, 2 * j], got[:, 2 * j + 1]
        out[j] = jnp.where(lane_ids(a) % 64 < 32, pltpu.roll(a, 96, 2), b)


def split(x):
    high = x.astype(jnp.bfloat16)
    return high, (x - high.astype(jnp.float32)).astype(jnp.bfloat16)


def dot3(a, b):
    dims = (((1,), (1,)), ((), ()))
    (ah, al), (bh, bl) = a, b
    parts = [
        lax.dot_general(x, y, dims, preferred_element_type=jnp.float32) for x, y in ((ah, bh), (ah, bl), (al, bh))
    ]
    return parts[0] + (parts[1] + parts[2])


def orbital_rows(a, b):
    low = lane_ids(a) < 64
    top = jnp.where(low, a, pltpu.roll(b, 64, 2))
    end = jnp.where(low, pltpu.roll(a, 64, 2), b)
    return jnp.stack([top, end], axis=1).reshape(-1, a.shape[-1])


def gram_own(got, half_diag, u, over, half, first, last, kept, done):
    keep = pltpu.make_async_copy(u, kept, done)
    keep.start()
    bands, depth, octet, _ = got.shape
    start = pl.multiple_of(lax.axis_index("y") * depth, 16)
    lane = lane_ids(got[:, 0])
    x = lane % 16
    z = lane % 64 // 16

    def one_sided(y):
        u = got[:, y]
        near = jnp.where(x < 15, pltpu.roll(u, 127, 2), pltpu.roll(u, 15, 2))
        far = jnp.where(x < 14, pltpu.roll(u, 126, 2), pltpu.roll(u, 14, 2))
        if y + 1 < depth:
            near = near + got[:, y + 1]
        if y + 2 < depth:
            far = far + got[:, y + 2]
        near = near + jnp.where(z >= 1, pltpu.roll(u, 16, 2), 0.0)
        far = far + jnp.where(z >= 2, pltpu.roll(u, 32, 2), 0.0)
        return half_diag[pl.ds(start + y, 1), :][None] * u + NEAR * near + FAR * far

    total_over, total_half = 0.0, 0.0
    for y in range(0, depth, 2):
        u = split(orbital_rows(got[:, y], got[:, y + 1]))
        w = split(orbital_rows(one_sided(y), one_sided(y + 1)))
        total_over = total_over + dot3(u, u)
        total_half = total_half + dot3(u, w)
    over[...] = total_over
    half[...] = total_half
    for j in range(first.shape[0]):
        two = []
        for y in (4 * j, 4 * j + 2):
            two.append(jnp.where(lane % 64 < 32, got[:, y], pltpu.roll(got[:, y + 1], 32, 2)))
        first[j] = orbital_rows(*two)
    last[...] = orbital_rows(got[:, depth - 2], got[:, depth - 1])
    keep.wait()


def gram_edge(edge, head, first, last, over, half, out):
    bands = edge.shape[1]
    third = lane_ids(edge[0]) % 32 < 16
    total = half[...]
    for j in range(first.shape[0]):
        two = []
        for e in (edge[2 * j], edge[2 * j + 1]):
            two.append(FAR * e + jnp.where(third, NEAR * pltpu.roll(e, 112, 2), 0.0))
        total = total + dot3(split(first[j]), split(orbital_rows(*two)))
    one, two = head[:, 0], head[:, 1]
    total = total + dot3(split(last[...]), split(orbital_rows(FAR * one, NEAR * one + FAR * two)))
    out[:, 0] = over[...].reshape(bands, -1, total.shape[-1])
    out[:, 1] = (total + total.T).reshape(bands, -1, total.shape[-1])


def call(body, out_shapes, *args, kept=0, scratch=(), flops=0):
    places = [VMEM] * (len(out_shapes) - kept) + [pl.BlockSpec(memory_space=pl.ANY)] * kept
    return pl.pallas_call(
        body,
        out_shape=[jax.ShapeDtypeStruct(s, jnp.float32) for s in out_shapes],
        in_specs=[VMEM] * len(args),
        out_specs=places,
        scratch_shapes=scratch,
        compiler_params=LIMIT,
        cost_estimate=pl.CostEstimate(flops=flops, bytes_accessed=1 << 20, transcendentals=0),
    )(*args)


def per_device(orbitals, potential):
    orbs, planes, rows, lanes = orbitals.shape
    slabs = lax.axis_size(GRID)
    bands = lax.axis_size("y")
    cells_all = slabs * planes * rows * lanes
    following = ring_shift(slabs, 1)
    outer = [(i, (i + (1 if i % 2 else -1)) % slabs) for i in range(slabs)]

    def both_sides(slab):
        off = lax.ppermute(slab, GRID, outer)
        return lax.ppermute(slab, "core", [(0, 1), (1, 0)]), off

    slab = jnp.concatenate([orbitals, potential[None]], axis=0)
    on, off = both_sides(slab)
    (own_xy,) = call(ahead_one, [orbitals.shape], slab, flops=1 << 28)
    g, diag = call(stage_one, [orbitals.shape, (planes + 4, rows, lanes)], slab, on, off, own_xy)
    on, off = both_sides(g)
    own_xy, half_diag = call(ahead_two, [orbitals.shape, (lanes, 2 * planes * rows)], g, diag, flops=1 << 28)
    total = bands * orbs
    u, send = call(
        stage_two,
        [orbitals.shape, (bands, lanes // bands, orbs // 2, 2 * planes * rows)],
        g,
        on,
        off,
        own_xy,
        slab,
        diag,
    )
    got = lax.all_to_all(send, "y", 0, 0, tiled=True)
    tile = (bands, orbs // 2, 2 * planes * rows)
    edge, head = call(pack_edge, [(lanes // bands // 2, *tile), (bands, 2, *tile[1:])], got)
    edge = lax.ppermute(edge, GRID, following)
    head = lax.ppermute(head, "y", ring_shift(bands, -1))
    firsts = (lanes // bands // 4, total, 2 * planes * rows)
    over, half, first, last, u = call(
        gram_own,
        [(total, total), (total, total), firsts, firsts[1:], u.shape],
        got,
        half_diag,
        u,
        kept=1,
        scratch=[pltpu.SemaphoreType.DMA],
        flops=1 << 30,
    )
    (part,) = call(gram_edge, [(bands, 2, orbs, total)], edge, head, first, last, over, half)

    pieces = lax.axis_size(REDUCERS)
    flat = part.reshape(pieces, -1, bands * orbs)
    mine = lax.all_to_all(flat, REDUCERS, 0, 0, tiled=True).sum(0)
    mine = lax.psum(mine, "core")
    spread = jnp.broadcast_to(mine[None], (slabs // 2, *mine.shape))
    back = lax.all_to_all(spread, ("x", "z"), 0, 0, tiled=True)
    both = back.reshape(lax.axis_size("x"), lax.axis_size("z"), *mine.shape).sum(1) / cells_all
    both = both.reshape(2, orbs, bands * orbs)
    return u, both[0], both[1]


def solution(mesh):
    devices = mesh.devices.reshape(4, 8, 2, 8)
    fine = Mesh(devices, ("x", "z", "core", "y"))
    in_specs = (P("y", GRID, None, None), P(GRID, None, None))
    out_specs = (P("y", GRID, None, None), P("y", None), P("y", None))
    return jax.shard_map(per_device, mesh=fine, in_specs=in_specs, out_specs=out_specs, check_vma=False)
```
